512 devices in a mesh: band: 16 (over z, core), tile: 32 (over y, x).
Axes of the slice: x: 4, y: 8, z: 8, core: 2. Of those that a mesh axis runs over, the one named last changes fastest.
Arguments:
- sources: bfloat16 [524288, 256], P(('band', 'tile')), may hold values from -6 to 6
- observed: bfloat16 [8192, 256], P('tile'), may hold values from -6 to 6
- v_factors: bfloat16 [8, 96, 524288], P(None, None, ('band', 'tile')), may hold values from -0.1875 to 0.1875
- u_factors: bfloat16 [512, 96, 8192], P('band', None, 'tile'), may hold values from -0.03125 to 0.03125
- tile_ranks: int32 [8, 512], P(None, ('band', 'tile')), may hold values from 32 to 96
- v_exponents: int32 [8, 512], P(None, ('band', 'tile')), may hold values from -1 to 1
- u_exponents: int32 [8, 512], P(None, ('band', 'tile')), may hold values from -1 to 1
Outputs:
- residual: float32 [8192, 256], P('tile', 'band')
- gradient: bfloat16 [524288, 256], P(('band', 'tile'))
The draws below stay inside these ranges and needn't reach their ends.
All inputs are finite; a program needn't handle non-finite values.
Results may differ from the reference program's by a relative error of at most 0.012.
Values may be sent and summed in bfloat16 or wider, within the bound.
A program may use at most 64 MiB of HBM per device.

```python
import jax
import jax.numpy as jnp
from jax import lax

B = 1024
S = 256
RMAX = 96
RMIN = 32
NR = 8
NCT = 512
NCOLS = 524288
ROWS = 8192
SLICE = 256
N_BAND = 16
N_TILE = 32


def set_ends(drawn, key, low, largest):
    extent = drawn.shape
    spot = [jax.random.randint(jax.random.fold_in(key, axis), (), 0, extent[axis]) for axis in range(len(extent))]
    drawn = drawn.at[tuple(spot)].set(low)
    longest = extent.index(max(extent))
    spot[longest] = (spot[longest] + 1) % extent[longest]
    return drawn.at[tuple(spot)].set(largest)


def steps_of(stream_key, shape, cuts, least, top_value):
    loudness, own = 1.0, jax.random.fold_in(stream_key, 6)
    for axis_at, shards_of in cuts:
        steps = jnp.exp(jax.random.uniform(jax.random.fold_in(own, axis_at), (shards_of,), jnp.float32, least / len(cuts), top_value / len(cuts)))
        loudness = loudness * jnp.repeat(steps, shape[axis_at] // shards_of).reshape([-1 if axis == axis_at else 1 for axis in range(len(shape))])
    return loudness


def gaussian(own_key, shape, deviation, most, split=(), kind=jnp.bfloat16):
    loudness = steps_of(own_key, shape, split, -0.22, 0.18) if split else 1.0
    result = jax.random.normal(own_key, shape, jnp.float32) * deviation * loudness
    return jnp.minimum(jnp.maximum(result, -most), most).astype(kind)


def setup_inputs(seed: int = 0) -> dict:
    keys = jax.random.split(jax.random.key(seed), 8)
    sources = gaussian(keys[0], (NCOLS, S), 1.0, 6.0, ((0, 512),))
    observed = gaussian(keys[1], (ROWS, S), 1.0, 6.0, ((0, 32),))
    v_factors = gaussian(keys[2], (NR, RMAX, NCOLS), B ** -0.5, 0.1875, ((2, 512),))
    u_factors = gaussian(keys[3], (NCT, RMAX, ROWS), (NCT * 64) ** -0.5, 0.03125, ((0, 16), (2, 32)))
    tile_ranks = set_ends(jax.random.randint(keys[4], (NR, NCT), RMIN, RMAX + 1), jax.random.fold_in(keys[4], 1), RMIN, RMAX).astype(jnp.int32)
    v_exponents = set_ends(jax.random.randint(keys[5], (NR, NCT), -1, 2), jax.random.fold_in(keys[5], 1), -1, 1).astype(jnp.int32)
    u_exponents = set_ends(jax.random.randint(keys[6], (NR, NCT), -1, 2), jax.random.fold_in(keys[6], 1), -1, 1).astype(jnp.int32)
    return dict(sources=sources, observed=observed, v_factors=v_factors, u_factors=u_factors, tile_ranks=tile_ranks, v_exponents=v_exponents, u_exponents=u_exponents)


def reference(sources, observed, v_factors, u_factors, tile_ranks, v_exponents, u_exponents):
    tile_count = N_BAND * N_TILE
    slices_per = N_TILE // NR
    rank_index = jnp.arange(RMAX, dtype=jnp.int32)
    weight = (rank_index[None, None, :] < tile_ranks[:, :, None]).astype(jnp.float32)
    weight = weight * jnp.exp2((v_exponents + u_exponents).astype(jnp.float32))[:, :, None]
    columns = jnp.arange(tile_count, dtype=jnp.int32)

    def forward(totals, column):
        v_tile = lax.dynamic_slice_in_dim(v_factors, column * B, B, 2).astype(jnp.float32)
        x_tile = lax.dynamic_slice_in_dim(sources, column * B, B, 0).astype(jnp.float32)
        pieces = jnp.einsum('ikb,bs->iks', v_tile, x_tile)
        tile_weights = lax.dynamic_index_in_dim(weight, column, 1, keepdims=False)
        pieces = (pieces * tile_weights[:, :, None]).astype(jnp.bfloat16)
        pieces = lax.optimization_barrier(pieces).astype(jnp.float32)
        u_tile = lax.dynamic_index_in_dim(u_factors, column, 0, keepdims=False).astype(jnp.float32)
        u_tile = u_tile.reshape(RMAX, NR, B)
        return totals + jnp.einsum('kib,iks->ibs', u_tile, pieces).reshape(ROWS, S), None

    product, _ = lax.scan(forward, jnp.zeros((ROWS, S), jnp.float32), columns)
    residual = product - observed.astype(jnp.float32)
    residual_rows = lax.optimization_barrier(residual.astype(jnp.bfloat16)).astype(jnp.float32)
    residual_rows = residual_rows.reshape(NR, slices_per, SLICE, S)

    def backward(carry, column):
        u_tile = lax.dynamic_index_in_dim(u_factors, column, 0, keepdims=False).astype(jnp.float32)
        u_tile = u_tile.reshape(RMAX, NR, slices_per, SLICE)
        partial_value = jnp.einsum('kiph,iphs->ipks', u_tile, residual_rows).astype(jnp.bfloat16)
        partial_value = lax.optimization_barrier(partial_value).astype(jnp.float32)
        tile_weights = lax.dynamic_index_in_dim(weight, column, 1, keepdims=False)
        adjoint = (jnp.sum(partial_value, axis=1) * tile_weights[:, :, None]).astype(jnp.bfloat16)
        v_tile = lax.dynamic_slice_in_dim(v_factors, column * B, B, 2).astype(jnp.float32)
        gradient_tile = jnp.einsum('ikb,iks->bs', v_tile, adjoint.astype(jnp.float32))
        return carry, gradient_tile.astype(jnp.bfloat16)

    _, gradient = lax.scan(backward, jnp.zeros((), jnp.float32), columns)
    return residual, gradient.reshape(NCOLS, S)
```

```python
import functools

import jax
import jax.numpy as jnp
from jax import lax
from jax.experimental import pallas as pl
from jax.experimental.pallas import tpu as pltpu
from jax.sharding import PartitionSpec as P

NX = 4
NH = 1
LAG = 2
F32, BF16 = jnp.float32, jnp.bfloat16
AR_TYPE = jnp.bfloat16


def displacements(ny):
    order = [0]
    for step in range(1, ny // 2 + 1):
        order.append(step)
        if ny - step != step:
            order.append(ny - step)
    return order


def dot(a, b):
    return jnp.dot(a, b, preferred_element_type=F32)


def kernel(
    ny, nb,
    src_hbm, obs_hbm, v_hbm, u_hbm, rank_ref, vexp_ref, uexp_ref,
    res_out, grad_out,
    src, obs, v, u, ut, vt, inc, out, acc,
    ar_out, ar_in, ag_out, ag_in, rows, res_t,
    part, via, comb, from_l, from_r, ys, ret, adj,
    load_sem, ysend, yrecv, xsend, xrecv, arsend, arrecv, agsend, agrecv, bsend, brecv, zsend, zrecv,
):
    tile = lax.axis_index("tile")
    band = lax.axis_index("band")
    y, x = tile // NX, tile % NX
    order = displacements(ny)
    rmax = v.shape[1]
    width = inc.shape[-1]
    rb = ar_out.shape[2]

    def mod(value, n):
        return lax.rem(value + n, n)

    xr, xl, xf = mod(x + 1, NX), mod(x - 1, NX), mod(x + 2, NX)
    right, left = {"tile": y * NX + xr}, {"tile": y * NX + xl}
    rows_to = [{"tile": mod(y + d, ny) * NX + x} for d in order]
    rows_back = [{"tile": mod(y - d, ny) * NX + x} for d in order]
    bands_to = [{"band": mod(band + j, nb)} for j in range(nb)]

    loads = [pltpu.make_async_copy(src_hbm, src, load_sem.at[0])]
    for p, d in enumerate(order):
        loads.append(pltpu.make_async_copy(v_hbm.at[mod(y + d, ny)], v.at[p], load_sem.at[1 + p]))
    for p, d in enumerate(order):
        first = pl.multiple_of(mod(y - d, ny) * NX, NX)
        loads.append(pltpu.make_async_copy(u_hbm.at[pl.ds(first, NX)], u.at[p], load_sem.at[1 + ny + p]))
    loads.append(pltpu.make_async_copy(obs_hbm, obs, load_sem.at[1 + 2 * ny]))
    for copy in loads:
        copy.start()

    barrier = pltpu.get_barrier_semaphore()
    peers = [right, left] + rows_to[1:] + bands_to[1:]
    for peer in peers:
        pl.semaphore_signal(barrier, inc=1, device_id=peer, device_id_type=pl.DeviceIdType.MESH)

    def remote(a, b, send, recv, to):
        return pltpu.make_async_remote_copy(
            src_ref=a, dst_ref=b, send_sem=send, recv_sem=recv, device_id=to,
            device_id_type=pl.DeviceIdType.MESH)

    sent = []

    def start(copy):
        copy.start()
        sent.append(copy)

    k_index = lax.broadcasted_iota(jnp.int32, (rmax, 1), 0)

    def weight(p):
        i = mod(y + order[p], ny)
        e = vexp_ref[i] + uexp_ref[i]
        scale = jnp.where(e == 2, 4.0, jnp.where(e == 1, 2.0, jnp.where(e == 0, 1.0, jnp.where(e == -1, 0.5, 0.25))))
        return jnp.where(k_index < rank_ref[i], scale.astype(F32), 0.0)

    def y_copy(h, p):
        return remote(out.at[h, p], inc.at[h, p, x], ysend.at[h, p], yrecv.at[h, p], rows_to[p])

    def x_copy(h, p, kind):
        if kind == 0:
            block, to = inc.at[h, p, x], right
        elif kind == 1:
            block, to = inc.at[h, p, x], left
        elif p % 2 == 0:
            block, to = inc.at[h, p, xl], right
        else:
            block, to = inc.at[h, p, xr], left
        return remote(block, block, xsend.at[h, p, kind], xrecv.at[h, p, kind], to)

    def x_wait(h, p, kind):
        slot = (xl, xr, xf)[kind]
        block = inc.at[h, p, slot]
        remote(block, block, xsend.at[h, p, kind], xrecv.at[h, p, kind], right).wait_recv()

    loads[0].wait()
    groups = [[0]] + [list(range(s, min(s + 2, ny))) for s in range(1, ny, 2)]
    for n, group in enumerate(groups):
        for p in group:
            loads[1 + p].wait()
        lhs = v[group[0]:group[-1] + 1].reshape(len(group) * rmax, v.shape[2])
        result = dot(lhs, src[...])
        for q, p in enumerate(group):
            piece = (result[q * rmax:(q + 1) * rmax] * weight(p)).astype(BF16)
            for h in range(NH):
                cut = piece[:, h * width:(h + 1) * width]
                if p == 0:
                    inc[h, 0, x] = cut
                else:
                    out[h, p] = cut
        if n == 0:
            pl.semaphore_wait(barrier, len(peers))
        for h in range(NH):
            for p in group:
                if p == 0:
                    if h == 0:
                        start(x_copy(h, 0, 0))
                        start(x_copy(h, 0, 1))
                else:
                    start(y_copy(h, p))

    def arrive(h, p):
        if p > 0:
            y_copy(h, p).wait_recv()
        if p > 0 or h > 0:
            start(x_copy(h, p, 0))
            start(x_copy(h, p, 1))

    def forward(h, p):
        x_wait(h, p, p % 2)
        start(x_copy(h, p, 2))

    def turn_u(p):
        loads[1 + ny + p].wait()
        ut[p] = u[p].reshape(NX * rmax, u.shape[3]).T

    def complete(h, p):
        x_wait(h, p, 1 - p % 2)
        x_wait(h, p, 2)
        term = dot(ut[p], inc[h, p].reshape(NX * rmax, width))
        if p == 0:
            acc[h] = term
        else:
            acc[h] += term

    def ar_copy(h, j):
        return remote(ar_out.at[h, mod(band + j, nb)], ar_in.at[h, j], arsend.at[h, j], arrecv.at[h, j], bands_to[j])

    def ag_copy(h, j):
        return remote(ag_out.at[h], ag_in.at[h, band], agsend.at[h, j], agrecv.at[h, j], bands_to[j])

    def reduce_send(h):
        ar_out[h] = acc[h].reshape(nb, rb, width).astype(AR_TYPE)
        for j in range(1, nb):
            start(ar_copy(h, j))

    def reduce_sum(h):
        mine = pl.ds(pl.multiple_of(band * rb, rb), rb)
        total = acc[h, mine, :] - obs[mine, h * width:(h + 1) * width].astype(F32)
        for j in range(1, nb):
            ar_copy(h, j).wait_recv()
            total = total + ar_in[h, j].astype(F32)
        total = total.astype(AR_TYPE)
        ag_out[h] = total
        ag_in[h, band] = total
        for j in range(1, nb):
            start(ag_copy(h, j))

    def reduce_done(h):
        for j in range(1, nb):
            block = ag_in.at[h, mod(band - j, nb)]
            remote(ag_out.at[h], block, agsend.at[h, j], agrecv.at[h, j], bands_to[j]).wait_recv()
        full = ag_in[h].reshape(nb * rb, width)
        rows[h] = full.astype(BF16)

    def residual(h):
        res_t[h * width:(h + 1) * width, :] = ag_in[h].reshape(nb * rb, width).astype(F32).T

    def hop_copy(h, p):
        return remote(part.at[h, p, xf], via.at[h, p], bsend.at[h, p, 2], brecv.at[h, p, 2], right if p % 2 == 0 else left)

    def plain_copy(h, p):
        if p % 2 == 0:
            return remote(part.at[h, p, xl], from_r.at[h, p], bsend.at[h, p, 1], brecv.at[h, p, 1], left)
        return remote(part.at[h, p, xr], from_l.at[h, p], bsend.at[h, p, 0], brecv.at[h, p, 0], right)

    def comb_copy(h, p):
        if p % 2 == 0:
            return remote(comb.at[h, p], from_l.at[h, p], bsend.at[h, p, 0], brecv.at[h, p, 0], right)
        return remote(comb.at[h, p], from_r.at[h, p], bsend.at[h, p, 1], brecv.at[h, p, 1], left)

    def z_copy(h, p):
        return remote(ys.at[h, p], ret.at[h, p], zsend.at[h, p], zrecv.at[h, p], rows_back[p])

    def spread(h, p):
        term = dot(u[p].reshape(NX * rmax, u.shape[3]), rows[h])
        part[h, p] = term.astype(BF16).reshape(NX, rmax, width)
        start(hop_copy(h, p))
        start(plain_copy(h, p))

    def combine(h, p):
        hop_copy(h, p).wait_recv()
        target = xr if p % 2 == 0 else xl
        comb[h, p] = (part[h, p, target].astype(F32) + via[h, p].astype(F32)).astype(BF16)
        start(comb_copy(h, p))

    def finish(h, p):
        plain_copy(h, p).wait_recv()
        comb_copy(h, p).wait_recv()
        total = part[h, p, x].astype(F32) + from_l[h, p].astype(F32) + from_r[h, p].astype(F32)
        if p == 0:
            ret[h, 0] = total.astype(BF16)
        else:
            ys[h, p] = total.astype(BF16)
            start(z_copy(h, p))

    def gather(h, p):
        if p > 0:
            z_copy(h, p).wait_recv()
        adj[h, p * rmax:(p + 1) * rmax, :] = (ret[h, p].astype(F32) * weight(p)).astype(BF16)

    def turn_v(g):
        lo, hi = g * ny // 2, (g + 1) * ny // 2
        vt[:, lo * rmax:hi * rmax] = v[lo:hi].reshape((hi - lo) * rmax, v.shape[2]).T

    for h in range(NH):
        for p in range(ny):
            arrive(h, p)
            if h == 0:
                turn_u(p)
            if p >= LAG:
                forward(h, p - LAG)
        for p in range(ny - LAG, ny):
            forward(h, p)
        for p in range(ny):
            complete(h, p)
        if h == 0:
            loads[1 + 2 * ny].wait()
        reduce_send(h)
        if h == 0:
            turn_v(0)
        reduce_sum(h)
        if h == 0:
            turn_v(1)
        reduce_done(h)
    back = list(range(ny - 1, -1, -1))
    for h in range(NH):
        for n, p in enumerate(back):
            spread(h, p)
            if n >= LAG:
                combine(h, back[n - LAG])
        for p in back[ny - LAG:]:
            combine(h, p)
        residual(h)
        for p in back:
            finish(h, p)
    mine = pl.ds(pl.multiple_of(band * res_out.shape[0], res_out.shape[0]), res_out.shape[0])
    res_out[...] = res_t[mine, :]
    for h in range(NH):
        for p in back:
            gather(h, p)
        grad_out[:, h * width:(h + 1) * width] = dot(vt[...], adj[h]).astype(BF16)
    for copy in sent:
        copy.wait_send()


def local(sources, observed, v_factors, u_factors, tile_ranks, v_exponents, u_exponents):
    nt, nb = lax.axis_size("tile"), lax.axis_size("band")
    ny = nt // NX
    nr, rmax, b = v_factors.shape
    nrow, s = observed.shape
    width, rb = s // NH, nrow // nb
    any_space = pl.BlockSpec(memory_space=pl.ANY)
    smem = pl.BlockSpec(memory_space=pltpu.SMEM)
    vmem = pl.BlockSpec(memory_space=pltpu.VMEM)
    sem = pltpu.SemaphoreType.DMA
    res, grad = pl.pallas_call(
        functools.partial(kernel, ny, nb),
        out_shape=(
            jax.ShapeDtypeStruct((s // nb, nrow), F32),
            jax.ShapeDtypeStruct((b, s), BF16),
        ),
        in_specs=[any_space] * 4 + [smem] * 3,
        out_specs=(vmem, vmem),
        scratch_shapes=[
            pltpu.VMEM((b, s), BF16),
            pltpu.VMEM((nrow, s), BF16),
            pltpu.VMEM((ny, rmax, b), BF16),
            pltpu.VMEM((ny, NX, rmax, nrow), BF16),
            pltpu.VMEM((ny, nrow, NX * rmax), BF16),
            pltpu.VMEM((b, ny * rmax), BF16),
            pltpu.VMEM((NH, ny, NX, rmax, width), BF16),
            pltpu.VMEM((NH, ny, rmax, width), BF16),
            pltpu.VMEM((NH, nrow, width), F32),
            pltpu.VMEM((NH, nb, rb, width), AR_TYPE),
            pltpu.VMEM((NH, nb, rb, width), AR_TYPE),
            pltpu.VMEM((NH, rb, width), AR_TYPE),
            pltpu.VMEM((NH, nb, rb, width), AR_TYPE),
            pltpu.VMEM((NH, nrow, width), BF16),
            pltpu.VMEM((s, nrow), F32),
            pltpu.VMEM((NH, ny, NX, rmax, width), BF16),
        ] + [pltpu.VMEM((NH, ny, rmax, width), BF16)] * 6 + [
            pltpu.VMEM((NH, ny * rmax, width), BF16),
            sem((2 + 2 * ny,)),
            sem((NH, ny)), sem((NH, ny)),
            sem((NH, ny, 3)), sem((NH, ny, 3)),
            sem((NH, nb)), sem((NH, nb)),
            sem((NH, nb)), sem((NH, nb)),
            sem((NH, ny, 3)), sem((NH, ny, 3)),
            sem((NH, ny)), sem((NH, ny)),
        ],
        compiler_params=pltpu.CompilerParams(
            collective_id=0, has_side_effects=True, vmem_limit_bytes=48 * 1024 * 1024),
        cost_estimate=pl.CostEstimate(flops=1_600_000_000, bytes_accessed=5_000_000, transcendentals=0),
    )(sources, observed, v_factors, u_factors,
      tile_ranks.reshape(-1), v_exponents.reshape(-1), u_exponents.reshape(-1))
    return res.T, grad


def solution(mesh):
    in_specs = (
        P(("band", "tile"), None),
        P("tile", None),
        P(None, None, ("band", "tile")),
        P("band", None, "tile"),
        P(None, ("band", "tile")),
        P(None, ("band", "tile")),
        P(None, ("band", "tile")),
    )
    out_specs = (P("tile", "band"), P(("band", "tile"), None))
    return jax.shard_map(local, mesh=mesh, in_specs=in_specs, out_specs=out_specs, check_vma=False)
```

```python
import functools

import jax
import jax.numpy as jnp
from jax import lax
from jax.experimental import pallas as pl
from jax.experimental.pallas import tpu as pltpu
from jax.sharding import PartitionSpec as P

NX = 4
NH = 2
F32, BF16 = jnp.float32, jnp.bfloat16
AR_TYPE = jnp.bfloat16


def displacements(ny):
    order, groups = [0], [[0]]
    for step in range(1, ny // 2 + 1):
        group = [step] if ny - step == step else [step, ny - step]
        groups.append(list(range(len(order), len(order) + len(group))))
        order += group
    return order, groups


def dot(a, b):
    return jnp.dot(a, b, preferred_element_type=F32)


def kernel(
    ny, nb,
    src_hbm, obs_hbm, v_hbm, u_hbm, rank_hbm, vexp_hbm, uexp_hbm,
    res_out, adj_out,
    rank_ref, vexp_ref, uexp_ref, src, obs, v, u, ut, inc, out, acc,
    ar_out, ar_in, ag_out, ag_in, rows, res_t,
    part, via, comb, from_l, from_r, ys, ret,
    load_sem, v_sem, u_sem, ysend, yrecv, xsend, xown, xfwd, arsend, arrecv, agsend, agrecv,
    bsend, bhop, brest, zsend, zrecv,
):
    tile = lax.axis_index("tile")
    band = lax.axis_index("band")
    y, x = tile // NX, tile % NX
    order, groups = displacements(ny)
    ng = len(groups)
    rmax = v.shape[1]
    width = inc.shape[-1]
    rb = ar_out.shape[2]
    nrow = u.shape[3]

    def mod(value, n):
        return lax.rem(value + n, n)

    xr, xl, xf = mod(x + 1, NX), mod(x - 1, NX), mod(x + 2, NX)
    right, left = {"tile": y * NX + xr}, {"tile": y * NX + xl}
    rows_to = [{"tile": mod(y + d, ny) * NX + x} for d in order]
    rows_back = [{"tile": mod(y - d, ny) * NX + x} for d in order]
    bands_to = [{"band": mod(band + j, nb)} for j in range(nb)]
    band_order = sorted(range(1, nb), key=lambda j: -min(j, nb - j))

    barrier = pltpu.get_barrier_semaphore()
    peers = [right, left] + rows_to[1:] + bands_to[1:]
    for peer in peers:
        pl.semaphore_signal(barrier, inc=1, device_id=peer, device_id_type=pl.DeviceIdType.MESH)

    v_groups = [[0, 1, 2], [5, 6, 7], [3, 4]] if ny == 8 else groups

    def v_copy(p):
        n = [p in group for group in v_groups].index(True)
        return pltpu.make_async_copy(v_hbm.at[mod(y + order[p], ny)], v.at[p], v_sem.at[n])

    def u_copy(g, p):
        first = pl.multiple_of(mod(y - order[p], ny) * NX, NX)
        return pltpu.make_async_copy(u_hbm.at[pl.ds(first, NX)], u.at[:, p], u_sem.at[g])

    small = [
        pltpu.make_async_copy(a, b, load_sem.at[n])
        for n, (a, b) in enumerate(((rank_hbm, rank_ref), (vexp_hbm, vexp_ref), (uexp_hbm, uexp_ref)))
    ]
    load_src = pltpu.make_async_copy(src_hbm, src, load_sem.at[3])
    load_obs = pltpu.make_async_copy(obs_hbm, obs, load_sem.at[4])
    load_src.start()
    for p in v_groups[0]:
        v_copy(p).start()
    for copy in small:
        copy.start()
    for group in v_groups[1:]:
        for p in group:
            v_copy(p).start()
    for g in range(ng):
        for p in groups[g]:
            u_copy(g, p).start()
    load_obs.start()

    def remote(a, b, send, recv, to):
        return pltpu.make_async_remote_copy(
            src_ref=a, dst_ref=b, send_sem=send, recv_sem=recv, device_id=to,
            device_id_type=pl.DeviceIdType.MESH)

    def arrived(ref, send, recv):
        remote(ref, ref, send, recv, right).wait_recv()

    def left_here(ref, send, recv):
        remote(ref, ref, send, recv, right).wait_send()

    k_index = lax.broadcasted_iota(jnp.int32, (rmax, 1), 0)

    def weight(p):
        i = mod(y + order[p], ny)
        e = vexp_ref[i] + uexp_ref[i]
        scale = jnp.where(e == 2, 4.0, jnp.where(e == 1, 2.0, jnp.where(e == 0, 1.0, jnp.where(e == -1, 0.5, 0.25))))
        return jnp.where(k_index < rank_ref[i], scale.astype(F32), 0.0)

    def span(g):
        return slice(groups[g][0], groups[g][-1] + 1)

    def group_of(p):
        return [p in group for group in groups].index(True)

    def y_start(h, p):
        remote(out.at[h, p - 1], inc.at[h, x, p], ysend.at[0], yrecv.at[h, group_of(p)], rows_to[p]).start()

    def own_start(h, g):
        block = inc.at[h, x, span(g)]
        remote(block, block, xsend.at[0], xown.at[h, g], right).start()
        remote(block, block, xsend.at[0], xown.at[h, g], left).start()

    load_src.wait()
    for n, group in enumerate(v_groups):
        cut = slice(group[0], group[-1] + 1)
        pltpu.make_async_copy(v.at[cut], v.at[cut], v_sem.at[n]).wait()
        result = dot(v[cut].reshape(len(group) * rmax, v.shape[2]), src[...])
        if n == 0:
            for copy in small:
                copy.wait()
        for q, p in enumerate(group):
            piece = (result[q * rmax:(q + 1) * rmax] * weight(p)).astype(BF16)
            for h in range(NH):
                half = piece[:, h * width:(h + 1) * width]
                if p == 0:
                    inc[h, x, 0] = half
                else:
                    out[h, p - 1] = half
        if n == 0:
            pl.semaphore_wait(barrier, len(peers))
            own_start(0, 0)
            own_start(1, 0)
        for p in group:
            if p > 0:
                y_start(0, p)

    def arrive(h, g):
        if g > 0:
            arrived(inc.at[h, 0, span(g)], ysend.at[0], yrecv.at[h, g])
        if g > 0:
            own_start(h, g)
        if h + 1 < NH:
            for p in groups[g]:
                if p > 0:
                    y_start(h + 1, p)

    def forward(h, g):
        arrived(inc.at[h, 0:2, span(g)], xsend.at[0], xown.at[h, g])
        for p in groups[g]:
            block = inc.at[h, xl if p % 2 == 0 else xr, p]
            remote(block, block, xsend.at[0], xfwd.at[h, g], right if p % 2 == 0 else left).start()

    def k_span(g):
        return slice(groups[g][0] * NX * rmax, (groups[g][-1] + 1) * NX * rmax)

    def turn_u(g):
        block = u.at[:, span(g)]
        pltpu.make_async_copy(block, block, u_sem.at[g]).wait()
        ut[:, k_span(g)] = u[:, span(g)].reshape(-1, nrow).T

    def complete(h, g):
        arrived(inc.at[h, 0, span(g)], xsend.at[0], xfwd.at[h, g])
        term = dot(ut[:, k_span(g)], inc[h, :, span(g)].reshape(-1, width))
        if g == 0:
            acc[h] = term
        else:
            acc[h] += term

    def reduce_send(h):
        ar_out[h] = acc[h].reshape(nb, rb, width).astype(AR_TYPE)
        for j in band_order:
            remote(ar_out.at[h, mod(band + j, nb)], ar_in.at[h, j], arsend.at[0], arrecv.at[h], bands_to[j]).start()

    def reduce_sum(h):
        mine = pl.ds(pl.multiple_of(band * rb, rb), rb)
        total = acc[h, mine, :] - obs[mine, h * width:(h + 1) * width].astype(F32)
        arrived(ar_in.at[h, 1:nb], arsend.at[0], arrecv.at[h])
        for j in range(1, nb):
            total = total + ar_in[h, j].astype(F32)
        total = total.astype(AR_TYPE)
        ag_out[h] = total
        ag_in[h, band] = total
        for j in band_order:
            remote(ag_out.at[h], ag_in.at[h, band], agsend.at[0], agrecv.at[h], bands_to[j]).start()

    def reduce_done(h):
        arrived(ar_in.at[h, 1:nb], agsend.at[0], agrecv.at[h])
        rows[h] = ag_in[h].reshape(nb * rb, width).astype(BF16)

    def residual(h):
        res_t[h * width:(h + 1) * width, :] = ag_in[h].reshape(nb * rb, width).astype(F32).T

    def hop_start(h, p):
        remote(part.at[h, xf, p], via.at[h, p], bsend.at[0], bhop.at[h, group_of(p)],
               right if p % 2 == 0 else left).start()

    def plain_start(h, p):
        if p % 2 == 0:
            remote(part.at[h, xl, p], from_r.at[h, p], bsend.at[0], brest.at[h, group_of(p)], left).start()
        else:
            remote(part.at[h, xr, p], from_l.at[h, p], bsend.at[0], brest.at[h, group_of(p)], right).start()

    def spread(h, g):
        term = dot(u[:, span(g)].reshape(-1, nrow), rows[h])
        part[h, :, span(g)] = term.astype(BF16).reshape(NX, len(groups[g]), rmax, width)
        for p in groups[g]:
            hop_start(h, p)

    def combine(h, g):
        arrived(via.at[h, span(g)], bsend.at[0], bhop.at[h, g])
        for p in groups[g]:
            target = xr if p % 2 == 0 else xl
            comb[h, p] = (part[h, target, p].astype(F32) + via[h, p].astype(F32)).astype(BF16)
            remote(comb.at[h, p], (from_l if p % 2 == 0 else from_r).at[h, p], bsend.at[0], brest.at[h, g],
                   right if p % 2 == 0 else left).start()

    def finish(h, g):
        arrived(part.at[h, 0:2, span(g)], bsend.at[0], brest.at[h, g])
        for p in groups[g]:
            total = part[h, x, p].astype(F32) + from_l[h, p].astype(F32) + from_r[h, p].astype(F32)
            if p == 0:
                ret[h, 0] = total.astype(BF16)
            else:
                ys[h, p - 1] = total.astype(BF16)
                remote(ys.at[h, p - 1], ret.at[h, p], zsend.at[0], zrecv.at[h, g], rows_back[p]).start()

    def gather(h, g):
        if g > 0:
            arrived(ret.at[h, span(g)], zsend.at[0], zrecv.at[h, g])
        for p in groups[g]:
            adj_out[mod(y + order[p], ny), :, h * width:(h + 1) * width] = (
                ret[h, p].astype(F32) * weight(p)).astype(BF16)

    back = list(range(ng - 1, -1, -1))

    def spread_all(h):
        for n, g in enumerate(back):
            spread(h, g)
            if n > 0:
                for p in groups[back[n - 1]]:
                    plain_start(h, p)
        for p in groups[back[-1]]:
            plain_start(h, p)

    arrive(0, 0)
    arrive(0, 1)
    turn_u(0)
    turn_u(1)
    arrive(0, 2)
    forward(0, 0)
    turn_u(2)
    arrive(0, 3)
    forward(0, 1)
    arrive(0, 4)
    turn_u(3)
    turn_u(4)
    forward(0, 2)
    arrive(1, 1)
    forward(0, 3)
    arrive(1, 2)
    complete(0, 0)
    complete(0, 1)
    forward(0, 4)
    arrive(1, 3)
    complete(0, 2)
    complete(0, 3)
    arrive(1, 4)
    complete(0, 4)
    load_obs.wait()
    reduce_send(0)
    forward(1, 0)
    forward(1, 1)
    forward(1, 2)
    forward(1, 3)
    forward(1, 4)
    complete(1, 0)
    complete(1, 1)
    complete(1, 2)
    complete(1, 3)
    reduce_sum(0)
    complete(1, 4)
    reduce_send(1)
    reduce_sum(1)
    reduce_done(0)
    spread_all(0)
    residual(0)
    for g in back:
        combine(0, g)
    reduce_done(1)
    spread_all(1)
    for g in back:
        finish(0, g)
    for g in back:
        combine(1, g)
    residual(1)
    mine = pl.ds(pl.multiple_of(band * res_out.shape[0], res_out.shape[0]), res_out.shape[0])
    res_out[...] = res_t[mine, :]
    for g in back:
        gather(0, g)
    for g in back:
        finish(1, g)
    for g in back:
        gather(1, g)
    left_here(out, ysend.at[0], yrecv.at[0, 0])
    left_here(inc.at[:, 0:3], xsend.at[0], xown.at[0, 0])
    left_here(ar_in.at[:, 1:nb], arsend.at[0], arrecv.at[0])
    left_here(ar_in.at[:, 1:nb], agsend.at[0], agrecv.at[0])
    left_here(part.at[:, 0:3], bsend.at[0], bhop.at[0, 0])
    left_here(ys, zsend.at[0], zrecv.at[0, 0])


def last_kernel(v, adj, res, grad_out, res_out):
    k = v.shape[0] * v.shape[1]
    grad_out[...] = lax.dot_general(
        v[...].reshape(k, v.shape[2]), adj[...].reshape(k, adj.shape[2]), (((0,), (0,)), ((), ())),
        preferred_element_type=F32).astype(BF16)
    res_out[...] = res[...]


def local(sources, observed, v_factors, u_factors, tile_ranks, v_exponents, u_exponents):
    nt, nb = lax.axis_size("tile"), lax.axis_size("band")
    ny = nt // NX
    nr, rmax, b = v_factors.shape
    nrow, s = observed.shape
    width, rb = s // NH, nrow // nb
    ng = len(displacements(ny)[1])
    hbm = pl.BlockSpec(memory_space=pl.ANY)
    vmem = pl.BlockSpec(memory_space=pltpu.VMEM)
    sem = pltpu.SemaphoreType.DMA
    res, adj = pl.pallas_call(
        functools.partial(kernel, ny, nb),
        out_shape=(
            jax.ShapeDtypeStruct((s // nb, nrow), F32),
            jax.ShapeDtypeStruct((nr, rmax, s), BF16),
        ),
        in_specs=[hbm] * 7,
        out_specs=(vmem, vmem),
        scratch_shapes=[
            pltpu.SMEM((nr,), jnp.int32),
            pltpu.SMEM((nr,), jnp.int32),
            pltpu.SMEM((nr,), jnp.int32),
            pltpu.VMEM((b, s), BF16),
            pltpu.VMEM((nrow, s), BF16),
            pltpu.VMEM((ny, rmax, b), BF16),
            pltpu.VMEM((NX, ny, rmax, nrow), BF16),
            pltpu.VMEM((nrow, ny * NX * rmax), BF16),
            pltpu.VMEM((NH, NX, ny, rmax, width), BF16),
            pltpu.VMEM((NH, ny - 1, rmax, width), BF16),
            pltpu.VMEM((NH, nrow, width), F32),
            pltpu.VMEM((NH, nb, rb, width), AR_TYPE),
            pltpu.VMEM((NH, nb, rb, width), AR_TYPE),
            pltpu.VMEM((NH, rb, width), AR_TYPE),
            pltpu.VMEM((NH, nb, rb, width), AR_TYPE),
            pltpu.VMEM((NH, nrow, width), BF16),
            pltpu.VMEM((s, nrow), F32),
            pltpu.VMEM((NH, NX, ny, rmax, width), BF16),
            pltpu.VMEM((NH, ny, rmax, width), BF16),
            pltpu.VMEM((NH, ny, rmax, width), BF16),
            pltpu.VMEM((NH, ny, rmax, width), BF16),
            pltpu.VMEM((NH, ny, rmax, width), BF16),
            pltpu.VMEM((NH, ny - 1, rmax, width), BF16),
            pltpu.VMEM((NH, ny, rmax, width), BF16),
            sem((5,)), sem((ng,)), sem((ng,)),
            sem((1,)), sem((NH, ng)),
            sem((1,)), sem((NH, ng)), sem((NH, ng)),
            sem((1,)), sem((NH,)),
            sem((1,)), sem((NH,)),
            sem((1,)), sem((NH, ng)), sem((NH, ng)),
            sem((1,)), sem((NH, ng)),
        ],
        compiler_params=pltpu.CompilerParams(
            collective_id=0, has_side_effects=True, vmem_limit_bytes=60 * 1024 * 1024),
        cost_estimate=pl.CostEstimate(flops=1_600_000_000, bytes_accessed=5_000_000, transcendentals=0),
    )(sources, observed, v_factors, u_factors,
      tile_ranks.reshape(-1), v_exponents.reshape(-1), u_exponents.reshape(-1))
    steps = 4
    grad, res = pl.pallas_call(
        last_kernel,
        grid=(steps,),
        out_shape=(jax.ShapeDtypeStruct((b, s), BF16), jax.ShapeDtypeStruct(res.shape, F32)),
        in_specs=[
            pl.BlockSpec((nr, rmax, b // steps), lambda i: (0, 0, i)),
            pl.BlockSpec(adj.shape, lambda i: (0, 0, 0)),
            pl.BlockSpec(res.shape, lambda i: (0, 0)),
        ],
        out_specs=(
            pl.BlockSpec((b // steps, s), lambda i: (i, 0)),
            pl.BlockSpec(res.shape, lambda i: (0, 0)),
        ),
        compiler_params=pltpu.CompilerParams(vmem_limit_bytes=62 * 1024 * 1024),
    )(v_factors, adj, res)
    return res.T, grad


def solution(mesh):
    in_specs = (
        P(("band", "tile"), None),
        P("tile", None),
        P(None, None, ("band", "tile")),
        P("band", None, "tile"),
        P(None, ("band", "tile")),
        P(None, ("band", "tile")),
        P(None, ("band", "tile")),
    )
    out_specs = (P("tile", "band"), P(("band", "tile"), None))
    return jax.shard_map(local, mesh=mesh, in_specs=in_specs, out_specs=out_specs, check_vma=False)
```

```python
import functools

import jax
import jax.numpy as jnp
from jax import lax
from jax.experimental import pallas as pl
from jax.experimental.pallas import tpu as pltpu
from jax.sharding import PartitionSpec as P

NX = 4
NH = 2
F32, BF16 = jnp.float32, jnp.bfloat16
AR_TYPE = jnp.bfloat16


def displacements(ny):
    order, groups = [0], [[0]]
    for step in range(1, ny // 2 + 1):
        group = [step] if ny - step == step else [step, ny - step]
        groups.append(list(range(len(order), len(order) + len(group))))
        order += group
    return order, groups


def dot(a, b):
    return jnp.dot(a, b, preferred_element_type=F32)


def kernel(
    ny, nb,
    src_hbm, obs_hbm, v_hbm, u_hbm, rank_hbm, vexp_hbm, uexp_hbm,
    res_out, adj_out,
    rank_ref, vexp_ref, uexp_ref, src, obs, v, u, ut, inc, out, acc,
    ar_out, ar_in, ag_out, ag_in, rows, res_t,
    part, via, comb, from_l, from_r, ys, ret,
    load_sem, v_sem, u_sem, ysend, yrecv, xsend, xown, xfwd, arsend, arrecv, agsend, agrecv,
    bsend, bhop, brest, zsend, zrecv,
):
    tile = lax.axis_index("tile")
    band = lax.axis_index("band")
    y, x = tile // NX, tile % NX
    order, groups = displacements(ny)
    ng = len(groups)
    rmax = v.shape[1]
    width = inc.shape[-1]
    rb = ar_out.shape[2]
    nrow = u.shape[3]

    def mod(value, n):
        return lax.rem(value + n, n)

    xr, xl, xf = mod(x + 1, NX), mod(x - 1, NX), mod(x + 2, NX)
    right, left = {"tile": y * NX + xr}, {"tile": y * NX + xl}
    rows_to = [{"tile": mod(y + d, ny) * NX + x} for d in order]
    rows_back = [{"tile": mod(y - d, ny) * NX + x} for d in order]
    bands_to = [{"band": mod(band + j, nb)} for j in range(nb)]
    band_order = sorted(range(1, nb), key=lambda j: -min(j, nb - j))

    v_groups = [[0, 1, 2], [5, 6, 7], [3, 4]] if ny == 8 else groups

    def v_copy(p):
        n = [p in group for group in v_groups].index(True)
        return pltpu.make_async_copy(v_hbm.at[mod(y + order[p], ny)], v.at[p], v_sem.at[n])

    def u_copy(g, p):
        first = pl.multiple_of(mod(y - order[p], ny) * NX, NX)
        return pltpu.make_async_copy(u_hbm.at[pl.ds(first, NX)], u.at[:, p], u_sem.at[g])

    small = [
        pltpu.make_async_copy(a, b, load_sem.at[n])
        for n, (a, b) in enumerate(((rank_hbm, rank_ref), (vexp_hbm, vexp_ref), (uexp_hbm, uexp_ref)))
    ]
    load_src = pltpu.make_async_copy(src_hbm, src, load_sem.at[3])
    load_obs = pltpu.make_async_copy(obs_hbm, obs, load_sem.at[4])
    load_src.start()
    for p in v_groups[0]:
        v_copy(p).start()
    for copy in small:
        copy.start()

    barrier = pltpu.get_barrier_semaphore()
    peers = [right, left] + rows_to[1:] + bands_to[1:]
    for peer in peers:
        pl.semaphore_signal(barrier, inc=1, device_id=peer, device_id_type=pl.DeviceIdType.MESH)

    for group in v_groups[1:]:
        for p in group:
            v_copy(p).start()
    for g in range(ng):
        for p in groups[g]:
            u_copy(g, p).start()
    load_obs.start()

    def remote(a, b, send, recv, to):
        return pltpu.make_async_remote_copy(
            src_ref=a, dst_ref=b, send_sem=send, recv_sem=recv, device_id=to,
            device_id_type=pl.DeviceIdType.MESH)

    def arrived(ref, send, recv):
        remote(ref, ref, send, recv, right).wait_recv()

    def left_here(ref, send, recv):
        remote(ref, ref, send, recv, right).wait_send()

    k_index = lax.broadcasted_iota(jnp.int32, (rmax, 1), 0)

    def weight(p):
        i = mod(y + order[p], ny)
        e = vexp_ref[i] + uexp_ref[i]
        scale = jnp.where(e == 2, 4.0, jnp.where(e == 1, 2.0, jnp.where(e == 0, 1.0, jnp.where(e == -1, 0.5, 0.25))))
        return jnp.where(k_index < rank_ref[i], scale.astype(F32), 0.0)

    def span(g):
        return slice(groups[g][0], groups[g][-1] + 1)

    def group_of(p):
        return [p in group for group in groups].index(True)

    def y_start(h, p):
        remote(out.at[h, p - 1], inc.at[h, x, p], ysend.at[0], yrecv.at[h, group_of(p)], rows_to[p]).start()

    def own_start(h, g):
        block = inc.at[h, x, span(g)]
        remote(block, block, xsend.at[0], xown.at[h, g], right).start()
        remote(block, block, xsend.at[0], xown.at[h, g], left).start()

    load_src.wait()
    for n, group in enumerate(v_groups):
        cut = slice(group[0], group[-1] + 1)
        pltpu.make_async_copy(v.at[cut], v.at[cut], v_sem.at[n]).wait()
        result = dot(v[cut].reshape(len(group) * rmax, v.shape[2]), src[...])
        if n == 0:
            for copy in small:
                copy.wait()
        for q, p in enumerate(group):
            piece = (result[q * rmax:(q + 1) * rmax] * weight(p)).astype(BF16)
            for h in range(NH):
                half = piece[:, h * width:(h + 1) * width]
                if p == 0:
                    inc[h, x, 0] = half
                else:
                    out[h, p - 1] = half
        if n == 0:
            pl.semaphore_wait(barrier, len(peers))
            own_start(0, 0)
            own_start(1, 0)
        for p in group:
            if p > 0:
                y_start(0, p)

    def arrive(h, g):
        if g > 0:
            arrived(inc.at[h, 0, span(g)], ysend.at[0], yrecv.at[h, g])
        if g > 0:
            own_start(h, g)
        if h + 1 < NH:
            for p in groups[g]:
                if p > 0:
                    y_start(h + 1, p)

    def forward(h, g):
        arrived(inc.at[h, 0:2, span(g)], xsend.at[0], xown.at[h, g])
        for p in groups[g]:
            block = inc.at[h, xl if p % 2 == 0 else xr, p]
            remote(block, block, xsend.at[0], xfwd.at[h, g], right if p % 2 == 0 else left).start()

    def k_span(g):
        return slice(groups[g][0] * NX * rmax, (groups[g][-1] + 1) * NX * rmax)

    def turn_u(g):
        block = u.at[:, span(g)]
        pltpu.make_async_copy(block, block, u_sem.at[g]).wait()
        ut[:, k_span(g)] = u[:, span(g)].reshape(-1, nrow).T

    def complete(h, g):
        arrived(inc.at[h, 0, span(g)], xsend.at[0], xfwd.at[h, g])
        term = dot(ut[:, k_span(g)], inc[h, :, span(g)].reshape(-1, width))
        if g == 0:
            acc[h] = term
        else:
            acc[h] += term

    def reduce_send(h):
        ar_out[h] = acc[h].reshape(nb, rb, width).astype(AR_TYPE)
        for j in band_order:
            remote(ar_out.at[h, mod(band + j, nb)], ar_in.at[h, j], arsend.at[0], arrecv.at[h], bands_to[j]).start()

    def reduce_sum(h):
        mine = pl.ds(pl.multiple_of(band * rb, rb), rb)
        total = acc[h, mine, :] - obs[mine, h * width:(h + 1) * width].astype(F32)
        arrived(ar_in.at[h, 1:nb], arsend.at[0], arrecv.at[h])
        for j in range(1, nb):
            total = total + ar_in[h, j].astype(F32)
        total = total.astype(AR_TYPE)
        ag_out[h] = total
        ag_in[h, band] = total
        for j in band_order:
            remote(ag_out.at[h], ag_in.at[h, band], agsend.at[0], agrecv.at[h], bands_to[j]).start()

    def reduce_done(h):
        arrived(ar_in.at[h, 1:nb], agsend.at[0], agrecv.at[h])
        rows[h] = ag_in[h].reshape(nb * rb, width).astype(BF16)

    def residual(h):
        res_t[h * width:(h + 1) * width, :] = ag_in[h].reshape(nb * rb, width).astype(F32).T

    def hop_start(h, p):
        remote(part.at[h, xf, p], via.at[h, p], bsend.at[0], bhop.at[h, group_of(p)],
               right if p % 2 == 0 else left).start()

    def plain_start(h, p):
        if p % 2 == 0:
            remote(part.at[h, xl, p], from_r.at[h, p], bsend.at[0], brest.at[h, group_of(p)], left).start()
        else:
            remote(part.at[h, xr, p], from_l.at[h, p], bsend.at[0], brest.at[h, group_of(p)], right).start()

    def spread(h, g):
        term = dot(u[:, span(g)].reshape(-1, nrow), rows[h])
        part[h, :, span(g)] = term.astype(BF16).reshape(NX, len(groups[g]), rmax, width)
        for p in groups[g]:
            hop_start(h, p)

    def combine(h, g):
        arrived(via.at[h, span(g)], bsend.at[0], bhop.at[h, g])
        for p in groups[g]:
            target = xr if p % 2 == 0 else xl
            comb[h, p] = (part[h, target, p].astype(F32) + via[h, p].astype(F32)).astype(BF16)
            remote(comb.at[h, p], (from_l if p % 2 == 0 else from_r).at[h, p], bsend.at[0], brest.at[h, g],
                   right if p % 2 == 0 else left).start()

    def finish(h, g):
        arrived(part.at[h, 0:2, span(g)], bsend.at[0], brest.at[h, g])
        for p in groups[g]:
            total = part[h, x, p].astype(F32) + from_l[h, p].astype(F32) + from_r[h, p].astype(F32)
            if p == 0:
                ret[h, 0] = total.astype(BF16)
            else:
                ys[h, p - 1] = total.astype(BF16)
                remote(ys.at[h, p - 1], ret.at[h, p], zsend.at[0], zrecv.at[h, g], rows_back[p]).start()

    def gather(h, g):
        if g > 0:
            arrived(ret.at[h, span(g)], zsend.at[0], zrecv.at[h, g])
        for p in groups[g]:
            adj_out[mod(y + order[p], ny), :, h * width:(h + 1) * width] = (
                ret[h, p].astype(F32) * weight(p)).astype(BF16)

    back = list(range(ng - 1, -1, -1))

    def spread_all(h):
        for n, g in enumerate(back):
            spread(h, g)
        for g in back:
            for p in groups[g]:
                plain_start(h, p)

    arrive(0, 0)
    arrive(0, 1)
    turn_u(0)
    turn_u(1)
    arrive(0, 2)
    forward(0, 0)
    turn_u(2)
    arrive(0, 3)
    forward(0, 1)
    arrive(0, 4)
    turn_u(3)
    turn_u(4)
    arrive(1, 1)
    forward(0, 2)
    arrive(1, 2)
    forward(0, 3)
    complete(0, 0)
    forward(0, 4)
    complete(0, 1)
    arrive(1, 3)
    complete(0, 2)
    arrive(1, 4)
    complete(0, 3)
    complete(0, 4)
    load_obs.wait()
    reduce_send(0)
    forward(1, 0)
    forward(1, 1)
    forward(1, 2)
    forward(1, 3)
    forward(1, 4)
    complete(1, 0)
    complete(1, 1)
    complete(1, 2)
    complete(1, 3)
    reduce_sum(0)
    complete(1, 4)
    reduce_send(1)
    reduce_done(0)
    spread_all(0)
    reduce_sum(1)
    residual(0)
    for g in back:
        combine(0, g)
    reduce_done(1)
    spread_all(1)
    for g in back:
        finish(0, g)
    for g in back:
        combine(1, g)
    residual(1)
    mine = pl.ds(pl.multiple_of(band * res_out.shape[0], res_out.shape[0]), res_out.shape[0])
    res_out[...] = res_t[mine, :]
    for g in back:
        gather(0, g)
    for g in back:
        finish(1, g)
    for g in back:
        gather(1, g)
    left_here(out, ysend.at[0], yrecv.at[0, 0])
    left_here(inc.at[:, 0:3], xsend.at[0], xown.at[0, 0])
    left_here(ar_in.at[:, 1:nb], arsend.at[0], arrecv.at[0])
    left_here(ar_in.at[:, 1:nb], agsend.at[0], agrecv.at[0])
    left_here(part.at[:, 0:3], bsend.at[0], bhop.at[0, 0])
    left_here(ys, zsend.at[0], zrecv.at[0, 0])


def last_kernel(v, adj, res, grad_out, res_out):
    k = v.shape[0] * v.shape[1]
    grad_out[...] = lax.dot_general(
        v[...].reshape(k, v.shape[2]), adj[...].reshape(k, adj.shape[2]), (((0,), (0,)), ((), ())),
        preferred_element_type=F32).astype(BF16)
    res_out[...] = res[...]


def local(sources, observed, v_factors, u_factors, tile_ranks, v_exponents, u_exponents):
    nt, nb = lax.axis_size("tile"), lax.axis_size("band")
    ny = nt // NX
    nr, rmax, b = v_factors.shape
    nrow, s = observed.shape
    width, rb = s // NH, nrow // nb
    ng = len(displacements(ny)[1])
    hbm = pl.BlockSpec(memory_space=pl.ANY)
    vmem = pl.BlockSpec(memory_space=pltpu.VMEM)
    sem = pltpu.SemaphoreType.DMA
    res, adj = pl.pallas_call(
        functools.partial(kernel, ny, nb),
        out_shape=(
            jax.ShapeDtypeStruct((s // nb, nrow), F32),
            jax.ShapeDtypeStruct((nr, rmax, s), BF16),
        ),
        in_specs=[hbm] * 7,
        out_specs=(vmem, vmem),
        scratch_shapes=[
            pltpu.SMEM((nr,), jnp.int32),
            pltpu.SMEM((nr,), jnp.int32),
            pltpu.SMEM((nr,), jnp.int32),
            pltpu.VMEM((b, s), BF16),
            pltpu.VMEM((nrow, s), BF16),
            pltpu.VMEM((ny, rmax, b), BF16),
            pltpu.VMEM((NX, ny, rmax, nrow), BF16),
            pltpu.VMEM((nrow, ny * NX * rmax), BF16),
            pltpu.VMEM((NH, NX, ny, rmax, width), BF16),
            pltpu.VMEM((NH, ny - 1, rmax, width), BF16),
            pltpu.VMEM((NH, nrow, width), F32),
            pltpu.VMEM((NH, nb, rb, width), AR_TYPE),
            pltpu.VMEM((NH, nb, rb, width), AR_TYPE),
            pltpu.VMEM((NH, rb, width), AR_TYPE),
            pltpu.VMEM((NH, nb, rb, width), AR_TYPE),
            pltpu.VMEM((NH, nrow, width), BF16),
            pltpu.VMEM((s, nrow), F32),
            pltpu.VMEM((NH, NX, ny, rmax, width), BF16),
            pltpu.VMEM((NH, ny, rmax, width), BF16),
            pltpu.VMEM((NH, ny, rmax, width), BF16),
            pltpu.VMEM((NH, ny, rmax, width), BF16),
            pltpu.VMEM((NH, ny, rmax, width), BF16),
            pltpu.VMEM((NH, ny - 1, rmax, width), BF16),
            pltpu.VMEM((NH, ny, rmax, width), BF16),
            sem((5,)), sem((ng,)), sem((ng,)),
            sem((1,)), sem((NH, ng)),
            sem((1,)), sem((NH, ng)), sem((NH, ng)),
            sem((1,)), sem((NH,)),
            sem((1,)), sem((NH,)),
            sem((1,)), sem((NH, ng)), sem((NH, ng)),
            sem((1,)), sem((NH, ng)),
        ],
        compiler_params=pltpu.CompilerParams(
            collective_id=0, has_side_effects=True, vmem_limit_bytes=60 * 1024 * 1024),
        cost_estimate=pl.CostEstimate(flops=1_600_000_000, bytes_accessed=5_000_000, transcendentals=0),
    )(sources, observed, v_factors, u_factors,
      tile_ranks.reshape(-1), v_exponents.reshape(-1), u_exponents.reshape(-1))
    steps = 2
    grad, res = pl.pallas_call(
        last_kernel,
        grid=(steps,),
        out_shape=(jax.ShapeDtypeStruct((b, s), BF16), jax.ShapeDtypeStruct(res.shape, F32)),
        in_specs=[
            pl.BlockSpec((nr, rmax, b // steps), lambda i: (0, 0, i)),
            pl.BlockSpec(adj.shape, lambda i: (0, 0, 0)),
            pl.BlockSpec(res.shape, lambda i: (0, 0)),
        ],
        out_specs=(
            pl.BlockSpec((b // steps, s), lambda i: (i, 0)),
            pl.BlockSpec(res.shape, lambda i: (0, 0)),
        ),
        compiler_params=pltpu.CompilerParams(vmem_limit_bytes=62 * 1024 * 1024),
    )(v_factors, adj, res)
    return res.T, grad


def solution(mesh):
    in_specs = (
        P(("band", "tile"), None),
        P("tile", None),
        P(None, None, ("band", "tile")),
        P("band", None, "tile"),
        P(None, ("band", "tile")),
        P(None, ("band", "tile")),
        P(None, ("band", "tile")),
    )
    out_specs = (P("tile", "band"), P(("band", "tile"), None))
    return jax.shard_map(local, mesh=mesh, in_specs=in_specs, out_specs=out_specs, check_vma=False)
```

```python
import functools

import jax
import jax.numpy as jnp
from jax import lax
from jax.experimental import pallas as pl
from jax.experimental.pallas import tpu as pltpu
from jax.sharding import PartitionSpec as P

NX = 4
NH = 2
F32, BF16 = jnp.float32, jnp.bfloat16
AR_TYPE = jnp.bfloat16


def displacements(ny):
    order, groups = [0], [[0]]
    for step in range(1, ny // 2 + 1):
        group = [step] if ny - step == step else [step, ny - step]
        groups.append(list(range(len(order), len(order) + len(group))))
        order += group
    return order, groups


def dot(a, b):
    return jnp.dot(a, b, preferred_element_type=F32)


def kernel(
    ny, nb,
    src_hbm, obs_hbm, v_hbm, u_hbm, rank_hbm, vexp_hbm, uexp_hbm,
    res_out, adj_out,
    rank_ref, vexp_ref, uexp_ref, src, obs, v, u, ut, inc, out, acc,
    ar_out, ar_in, ag_out, ag_in, rows, res_t,
    part, via, comb, from_l, from_r, ys, ret,
    load_sem, v_sem, u_sem, ysend, yrecv, xsend, xown, xfwd, arsend, arrecv, agsend, agrecv,
    bsend, bhop, brest, zsend, zrecv,
):
    tile = lax.axis_index("tile")
    band = lax.axis_index("band")
    y, x = tile // NX, tile % NX
    order, groups = displacements(ny)
    ng = len(groups)
    rmax = v.shape[1]
    width = inc.shape[-1]
    rb = ar_out.shape[2]
    nrow = u.shape[3]

    def mod(value, n):
        return lax.rem(value + n, n)

    xr, xl, xf = mod(x + 1, NX), mod(x - 1, NX), mod(x + 2, NX)
    right, left = {"tile": y * NX + xr}, {"tile": y * NX + xl}
    across = {"tile": y * NX + xf}
    rows_to = [{"tile": mod(y + d, ny) * NX + x} for d in order]
    rows_back = [{"tile": mod(y - d, ny) * NX + x} for d in order]
    bands_to = [{"band": mod(band + j, nb)} for j in range(nb)]
    band_order = sorted(range(1, nb), key=lambda j: -min(j, nb - j))

    v_groups = [[0, 1, 2], [5, 6, 7], [3, 4]] if ny == 8 else groups

    def v_copy(p):
        n = [p in group for group in v_groups].index(True)
        return pltpu.make_async_copy(v_hbm.at[mod(y + order[p], ny)], v.at[p], v_sem.at[n])

    def u_copy(g, p):
        first = pl.multiple_of(mod(y - order[p], ny) * NX, NX)
        return pltpu.make_async_copy(u_hbm.at[pl.ds(first, NX)], u.at[:, p], u_sem.at[g])

    small = [
        pltpu.make_async_copy(a, b, load_sem.at[n])
        for n, (a, b) in enumerate(((rank_hbm, rank_ref), (vexp_hbm, vexp_ref), (uexp_hbm, uexp_ref)))
    ]
    load_src = pltpu.make_async_copy(src_hbm, src, load_sem.at[3])
    load_obs = pltpu.make_async_copy(obs_hbm, obs, load_sem.at[4])
    load_src.start()
    for p in v_groups[0]:
        v_copy(p).start()
    for copy in small:
        copy.start()

    barrier = pltpu.get_barrier_semaphore()
    peers = [right, left, across] + rows_to[1:] + bands_to[1:]
    for peer in peers:
        pl.semaphore_signal(barrier, inc=1, device_id=peer, device_id_type=pl.DeviceIdType.MESH)

    for group in v_groups[1:]:
        for p in group:
            v_copy(p).start()

    def remote(a, b, send, recv, to):
        return pltpu.make_async_remote_copy(
            src_ref=a, dst_ref=b, send_sem=send, recv_sem=recv, device_id=to,
            device_id_type=pl.DeviceIdType.MESH)

    def arrived(ref, send, recv):
        remote(ref, ref, send, recv, right).wait_recv()

    def left_here(ref, send, recv):
        remote(ref, ref, send, recv, right).wait_send()

    k_index = lax.broadcasted_iota(jnp.int32, (rmax, 1), 0)

    def weight(p):
        i = mod(y + order[p], ny)
        e = vexp_ref[i] + uexp_ref[i]
        scale = jnp.where(e == 2, 4.0, jnp.where(e == 1, 2.0, jnp.where(e == 0, 1.0, jnp.where(e == -1, 0.5, 0.25))))
        return jnp.where(k_index < rank_ref[i], scale.astype(F32), 0.0)

    def span(g):
        return slice(groups[g][0], groups[g][-1] + 1)

    def group_of(p):
        return [p in group for group in groups].index(True)

    def y_start(h, p):
        remote(out.at[h, p - 1], inc.at[h, x, p], ysend.at[0], yrecv.at[h, group_of(p)], rows_to[p]).start()

    def own_start(h, g):
        block = inc.at[h, x, span(g)]
        remote(block, block, xsend.at[0], xown.at[h, g], right).start()
        remote(block, block, xsend.at[0], xown.at[h, g], left).start()
        if h == 0 and g == ng - 1:
            remote(block, block, xsend.at[0], xfwd.at[h, g], across).start()

    load_src.wait()
    for n, group in enumerate(v_groups):
        cut = slice(group[0], group[-1] + 1)
        pltpu.make_async_copy(v.at[cut], v.at[cut], v_sem.at[n]).wait()
        result = dot(v[cut].reshape(len(group) * rmax, v.shape[2]), src[...])
        if n == 0:
            for copy in small:
                copy.wait()
        for q, p in enumerate(group):
            piece = (result[q * rmax:(q + 1) * rmax] * weight(p)).astype(BF16)
            for h in range(NH):
                half = piece[:, h * width:(h + 1) * width]
                if p == 0:
                    inc[h, x, 0] = half
                else:
                    out[h, p - 1] = half
        if n == 0:
            pl.semaphore_wait(barrier, len(peers))
            own_start(0, 0)
            own_start(1, 0)
        for p in group:
            if p > 0:
                y_start(0, p)

    for g in range(ng):
        for p in groups[g]:
            u_copy(g, p).start()
    load_obs.start()

    def arrive(h, g):
        if g > 0:
            arrived(inc.at[h, 0, span(g)], ysend.at[0], yrecv.at[h, g])
        if g > 0:
            own_start(h, g)
        if h + 1 < NH:
            for p in groups[g]:
                if p > 0:
                    y_start(h + 1, p)

    def forward(h, g):
        if h == 0 and g == ng - 1:
            arrived(inc.at[h, 0:2, span(g)], xsend.at[0], xown.at[h, g])
            return
        arrived(inc.at[h, 0:2, span(g)], xsend.at[0], xown.at[h, g])
        for p in groups[g]:
            block = inc.at[h, xl if p % 2 == 0 else xr, p]
            remote(block, block, xsend.at[0], xfwd.at[h, g], right if p % 2 == 0 else left).start()

    def k_span(g):
        return slice(groups[g][0] * NX * rmax, (groups[g][-1] + 1) * NX * rmax)

    def turn_u(g):
        block = u.at[:, span(g)]
        pltpu.make_async_copy(block, block, u_sem.at[g]).wait()
        ut[:, k_span(g)] = u[:, span(g)].reshape(-1, nrow).T

    def complete(h, g):
        arrived(inc.at[h, 0, span(g)], xsend.at[0], xfwd.at[h, g])
        term = dot(ut[:, k_span(g)], inc[h, :, span(g)].reshape(-1, width))
        if g == 0:
            acc[h] = term
        else:
            acc[h] += term

    def reduce_send(h):
        ar_out[h] = acc[h].reshape(nb, rb, width).astype(AR_TYPE)
        for j in band_order:
            remote(ar_out.at[h, mod(band + j, nb)], ar_in.at[h, j], arsend.at[0], arrecv.at[h], bands_to[j]).start()

    def reduce_sum(h):
        mine = pl.ds(pl.multiple_of(band * rb, rb), rb)
        total = acc[h, mine, :] - obs[mine, h * width:(h + 1) * width].astype(F32)
        arrived(ar_in.at[h, 1:nb], arsend.at[0], arrecv.at[h])
        for j in range(1, nb):
            total = total + ar_in[h, j].astype(F32)
        total = total.astype(AR_TYPE)
        ag_out[h] = total
        ag_in[h, band] = total
        for j in band_order:
            remote(ag_out.at[h], ag_in.at[h, band], agsend.at[0], agrecv.at[h], bands_to[j]).start()

    def reduce_done(h):
        arrived(ar_in.at[h, 1:nb], agsend.at[0], agrecv.at[h])
        rows[h] = ag_in[h].reshape(nb * rb, width).astype(BF16)

    def residual(h):
        res_t[h * width:(h + 1) * width, :] = ag_in[h].reshape(nb * rb, width).astype(F32).T

    def hop_start(h, p):
        remote(part.at[h, xf, p], via.at[h, p], bsend.at[0], bhop.at[h, group_of(p)],
               right if p % 2 == 0 else left).start()

    def plain_start(h, p):
        if p % 2 == 0:
            remote(part.at[h, xl, p], from_r.at[h, p], bsend.at[0], brest.at[h, group_of(p)], left).start()
        else:
            remote(part.at[h, xr, p], from_l.at[h, p], bsend.at[0], brest.at[h, group_of(p)], right).start()

    def spread(h, g):
        term = dot(u[:, span(g)].reshape(-1, nrow), rows[h])
        part[h, :, span(g)] = term.astype(BF16).reshape(NX, len(groups[g]), rmax, width)
        for p in groups[g]:
            hop_start(h, p)

    def combine(h, g):
        arrived(via.at[h, span(g)], bsend.at[0], bhop.at[h, g])
        for p in groups[g]:
            target = xr if p % 2 == 0 else xl
            comb[h, p] = (part[h, target, p].astype(F32) + via[h, p].astype(F32)).astype(BF16)
            remote(comb.at[h, p], (from_l if p % 2 == 0 else from_r).at[h, p], bsend.at[0], brest.at[h, g],
                   right if p % 2 == 0 else left).start()

    def finish(h, g):
        arrived(part.at[h, 0:2, span(g)], bsend.at[0], brest.at[h, g])
        for p in groups[g]:
            total = part[h, x, p].astype(F32) + from_l[h, p].astype(F32) + from_r[h, p].astype(F32)
            if p == 0:
                ret[h, 0] = total.astype(BF16)
            else:
                ys[h, p - 1] = total.astype(BF16)
                remote(ys.at[h, p - 1], ret.at[h, p], zsend.at[0], zrecv.at[h], rows_back[p]).start()

    def gather(h, g):
        if g == ng - 1:
            arrived(ret.at[h, 1:ny], zsend.at[0], zrecv.at[h])
        for p in groups[g]:
            adj_out[mod(y + order[p], ny), :, h * width:(h + 1) * width] = (
                ret[h, p].astype(F32) * weight(p)).astype(BF16)

    back = list(range(ng - 1, -1, -1))

    def spread_all(h):
        for n, g in enumerate(back):
            spread(h, g)
        for g in back:
            for p in groups[g]:
                plain_start(h, p)

    arrive(0, 0)
    arrive(0, 1)
    turn_u(0)
    turn_u(1)
    arrive(0, 2)
    forward(0, 0)
    turn_u(2)
    arrive(0, 3)
    forward(0, 1)
    arrive(0, 4)
    turn_u(3)
    turn_u(4)
    arrive(1, 1)
    forward(0, 2)
    arrive(1, 2)
    forward(0, 3)
    complete(0, 0)
    forward(0, 4)
    complete(0, 1)
    arrive(1, 3)
    complete(0, 2)
    arrive(1, 4)
    complete(0, 3)
    complete(0, 4)
    load_obs.wait()
    reduce_send(0)
    forward(1, 0)
    forward(1, 1)
    forward(1, 2)
    forward(1, 3)
    forward(1, 4)
    complete(1, 0)
    complete(1, 1)
    complete(1, 2)
    complete(1, 3)
    reduce_sum(0)
    complete(1, 4)
    reduce_send(1)
    reduce_done(0)
    for g in back[:2]:
        spread(0, g)
    reduce_sum(1)
    for g in back[2:]:
        spread(0, g)
    for g in back:
        for p in groups[g]:
            plain_start(0, p)
    residual(0)
    for g in back:
        combine(0, g)
    reduce_done(1)
    for g in back:
        spread(1, g)
    for g in back[:2]:
        for p in groups[g]:
            plain_start(1, p)
    for g in back:
        finish(0, g)
    for g in back[:2]:
        combine(1, g)
    for g in back[2:]:
        for p in groups[g]:
            plain_start(1, p)
    for g in back[2:]:
        combine(1, g)
    residual(1)
    mine = pl.ds(pl.multiple_of(band * res_out.shape[0], res_out.shape[0]), res_out.shape[0])
    res_out[...] = res_t[mine, :]
    for g in back:
        finish(1, g)
    for g in back:
        gather(0, g)
    for g in back:
        gather(1, g)
    left_here(out, ysend.at[0], yrecv.at[0, 0])
    left_here(inc.at[:, 0:3], xsend.at[0], xown.at[0, 0])
    left_here(ar_in.at[:, 1:nb], arsend.at[0], arrecv.at[0])
    left_here(ar_in.at[:, 1:nb], agsend.at[0], agrecv.at[0])
    left_here(part.at[:, 0:3], bsend.at[0], bhop.at[0, 0])
    left_here(ys, zsend.at[0], zrecv.at[0])


def last_kernel(v, adj, res, grad_out, res_out):
    k = v.shape[0] * v.shape[1]
    grad_out[...] = lax.dot_general(
        v[...].reshape(k, v.shape[2]), adj[...].reshape(k, adj.shape[2]), (((0,), (0,)), ((), ())),
        preferred_element_type=F32).astype(BF16)
    res_out[...] = res[...]


def local(sources, observed, v_factors, u_factors, tile_ranks, v_exponents, u_exponents):
    nt, nb = lax.axis_size("tile"), lax.axis_size("band")
    ny = nt // NX
    nr, rmax, b = v_factors.shape
    nrow, s = observed.shape
    width, rb = s // NH, nrow // nb
    ng = len(displacements(ny)[1])
    hbm = pl.BlockSpec(memory_space=pl.ANY)
    vmem = pl.BlockSpec(memory_space=pltpu.VMEM)
    sem = pltpu.SemaphoreType.DMA
    res, adj = pl.pallas_call(
        functools.partial(kernel, ny, nb),
        out_shape=(
            jax.ShapeDtypeStruct((s // nb, nrow), F32),
            jax.ShapeDtypeStruct((nr, rmax, s), BF16),
        ),
        in_specs=[hbm] * 7,
        out_specs=(vmem, vmem),
        scratch_shapes=[
            pltpu.SMEM((nr,), jnp.int32),
            pltpu.SMEM((nr,), jnp.int32),
            pltpu.SMEM((nr,), jnp.int32),
            pltpu.VMEM((b, s), BF16),
            pltpu.VMEM((nrow, s), BF16),
            pltpu.VMEM((ny, rmax, b), BF16),
            pltpu.VMEM((NX, ny, rmax, nrow), BF16),
            pltpu.VMEM((nrow, ny * NX * rmax), BF16),
            pltpu.VMEM((NH, NX, ny, rmax, width), BF16),
            pltpu.VMEM((NH, ny - 1, rmax, width), BF16),
            pltpu.VMEM((NH, nrow, width), F32),
            pltpu.VMEM((NH, nb, rb, width), AR_TYPE),
            pltpu.VMEM((NH, nb, rb, width), AR_TYPE),
            pltpu.VMEM((NH, rb, width), AR_TYPE),
            pltpu.VMEM((NH, nb, rb, width), AR_TYPE),
            pltpu.VMEM((NH, nrow, width), BF16),
            pltpu.VMEM((s, nrow), F32),
            pltpu.VMEM((NH, NX, ny, rmax, width), BF16),
            pltpu.VMEM((NH, ny, rmax, width), BF16),
            pltpu.VMEM((NH, ny, rmax, width), BF16),
            pltpu.VMEM((NH, ny, rmax, width), BF16),
            pltpu.VMEM((NH, ny, rmax, width), BF16),
            pltpu.VMEM((NH, ny - 1, rmax, width), BF16),
            pltpu.VMEM((NH, ny, rmax, width), BF16),
            sem((5,)), sem((len(displacements(ny)[1]),)), sem((ng,)),
            sem((1,)), sem((NH, ng)),
            sem((1,)), sem((NH, ng)), sem((NH, ng)),
            sem((1,)), sem((NH,)),
            sem((1,)), sem((NH,)),
            sem((1,)), sem((NH, ng)), sem((NH, ng)),
            sem((1,)), sem((NH,)),
        ],
        compiler_params=pltpu.CompilerParams(
            collective_id=0, has_side_effects=True, vmem_limit_bytes=60 * 1024 * 1024),
        cost_estimate=pl.CostEstimate(flops=1_600_000_000, bytes_accessed=5_000_000, transcendentals=0),
    )(sources, observed, v_factors, u_factors,
      tile_ranks.reshape(-1), v_exponents.reshape(-1), u_exponents.reshape(-1))
    steps = 2
    grad, res = pl.pallas_call(
        last_kernel,
        grid=(steps,),
        out_shape=(jax.ShapeDtypeStruct((b, s), BF16), jax.ShapeDtypeStruct(res.shape, F32)),
        in_specs=[
            pl.BlockSpec((nr, rmax, b // steps), lambda i: (0, 0, i)),
            pl.BlockSpec(adj.shape, lambda i: (0, 0, 0)),
            pl.BlockSpec(res.shape, lambda i: (0, 0)),
        ],
        out_specs=(
            pl.BlockSpec((b // steps, s), lambda i: (i, 0)),
            pl.BlockSpec(res.shape, lambda i: (0, 0)),
        ),
        compiler_params=pltpu.CompilerParams(vmem_limit_bytes=62 * 1024 * 1024),
    )(v_factors, adj, res)
    return res.T, grad


def solution(mesh):
    in_specs = (
        P(("band", "tile"), None),
        P("tile", None),
        P(None, None, ("band", "tile")),
        P("band", None, "tile"),
        P(None, ("band", "tile")),
        P(None, ("band", "tile")),
        P(None, ("band", "tile")),
    )
    out_specs = (P("tile", "band"), P(("band", "tile"), None))
    return jax.shard_map(local, mesh=mesh, in_specs=in_specs, out_specs=out_specs, check_vma=False)
```
